512 devices in a mesh: dp: 16 (over z, core), vocab: 32 (over y, x).
Axes of the slice: x: 4, y: 8, z: 8, core: 2. Of those that a mesh axis runs over, the one named last changes fastest.
Arguments:
- student_hidden: bfloat16 [480, 2048], P('dp', 'vocab'), may hold values from -8 to 8
- teacher_hidden: bfloat16 [480, 4096], P('dp', 'vocab'), may hold values from -8 to 8
- student_head: bfloat16 [128000, 2048], P(('dp', 'vocab')), may hold values from -0.35 to 0.35
- teacher_head: bfloat16 [128000, 4096], P(('dp', 'vocab')), may hold values from -0.35 to 0.35
Outputs:
- loss: float32 [], replicated
- hidden_grad: float32 [480, 2048], P('dp', 'vocab')
- head_grad: bfloat16 [128000, 2048], P(('dp', 'vocab'))
The draws below stay inside these ranges and needn't reach their ends.
All inputs are finite; a program needn't handle non-finite values.
Results may differ from the reference program's by a relative error of at most 0.0046.
Values may be sent and summed in bfloat16 or wider, within the bound.
No kernel may reach another device: no remote copies, remote signals or barrier semaphores. Data moves between devices by JAX's collectives and lax.ppermute only.
A program may use at most 64 MiB of HBM per device.

```python
import math
import jax
import jax.numpy as jnp

D_S = 2048
D_T = 4096
TOKENS = 480
VOCAB = 128000


def teacher_rows(key):
    return jax.random.normal(jax.random.fold_in(key, 11), (VOCAB, D_T), jnp.float32)


def student_rows(key):
    return jax.random.normal(jax.random.fold_in(key, 12), (VOCAB, D_S), jnp.float32)


def drawn(key, salt):
    pairs = jax.random.randint(jax.random.fold_in(key, salt), (8,), 0, VOCAB // 2) * 2
    tokens_hit = jax.random.randint(jax.random.fold_in(key, salt + 1), (8,), 0, TOKENS)
    return (pairs.astype(jnp.int32), tokens_hit.astype(jnp.int32))


def near_pair(base, pairs, key, width):
    noise = jax.random.normal(key, (8, width), jnp.float32)
    return base.at[pairs + 1].set(0.99 * base[pairs] + 0.1 * noise)


def lifted(states, base, pairs, tokens_hit, strength, width):
    factor = 100.0 / (3.0 * math.sqrt(width))
    return states.at[tokens_hit].set((factor * strength)[:, None] * base[pairs])


def draw_teacher_head(key, part):
    base = teacher_rows(key)
    pairs, tokens_hit = drawn(key, 31)
    key = jax.random.fold_in(key, 21)
    base = near_pair(base, pairs, key, D_T)
    return jnp.clip(base * (3.0 / math.sqrt(D_T)), -0.35, 0.35).astype(jnp.bfloat16)


def draw_student_head(key, part):
    base = student_rows(key)
    pairs, tokens_hit = drawn(key, 41)
    key = jax.random.fold_in(key, 23)
    base = near_pair(base, pairs, key, D_S)
    return jnp.clip(base * (3.0 / math.sqrt(D_S)), -0.35, 0.35).astype(jnp.bfloat16)


def draw_teacher_hidden(key, part):
    base = teacher_rows(key)
    pairs, tokens_hit = drawn(key, 31)
    key = jax.random.fold_in(key, 22)
    states = jax.random.normal(key, (TOKENS, D_T), jnp.float32)
    strength = jnp.array([1.0, 1.6, 2.4, 1.0, 1.6, 2.4, 1.0, 1.6], jnp.float32)
    states = lifted(states, base, pairs, tokens_hit, strength, D_T)
    return jnp.clip(states, -8.0, 8.0).astype(jnp.bfloat16)


def draw_student_hidden(key, part):
    base = student_rows(key)
    pairs, tokens_hit = drawn(key, 41)
    key = jax.random.fold_in(key, 24)
    states = jax.random.normal(key, (TOKENS, D_S), jnp.float32)
    strength = jnp.array([1.0, 1.6, 2.4, 1.0, 1.6, 2.4, 1.0, 1.6], jnp.float32)
    states = lifted(states, base, pairs, tokens_hit, strength, D_S)
    return jnp.clip(states, -8.0, 8.0).astype(jnp.bfloat16)


def setup_inputs(seed: int = 0) -> dict:
    streams_of = jax.random.split(jax.random.key(seed), 5)
    student_hidden = draw_student_hidden(jax.random.fold_in(streams_of[4], 71), 0)
    teacher_hidden = draw_teacher_hidden(jax.random.fold_in(streams_of[4], 71), 0)
    student_head = draw_student_head(jax.random.fold_in(streams_of[4], 71), 0)
    teacher_head = draw_teacher_head(jax.random.fold_in(streams_of[4], 71), 0)
    return dict(student_hidden=student_hidden, teacher_hidden=teacher_hidden, student_head=student_head, teacher_head=teacher_head)


def reference(student_hidden, teacher_hidden, student_head, teacher_head):
    teacher_logits = jnp.dot(teacher_hidden, teacher_head.T, preferred_element_type=jnp.float32)
    student_logits = jnp.dot(student_hidden, student_head.T, preferred_element_type=jnp.float32)
    teacher_max = jnp.max(teacher_logits, axis=1, keepdims=True)
    student_max = jnp.max(student_logits, axis=1, keepdims=True)
    teacher_exp = jnp.exp(teacher_logits - teacher_max)
    teacher_total = jnp.sum(teacher_exp, axis=1, keepdims=True)
    student_total = jnp.sum(jnp.exp(student_logits - student_max), axis=1, keepdims=True)
    cross = jnp.sum(teacher_exp * (teacher_logits - student_logits), axis=1, keepdims=True)
    teacher_lse = teacher_max + jnp.log(teacher_total)
    student_lse = student_max + jnp.log(student_total)
    kl = cross / teacher_total - teacher_lse + student_lse
    loss = jnp.mean(kl)
    logit_grad = (jnp.exp(student_logits - student_lse) - jnp.exp(teacher_logits - teacher_lse)).astype(jnp.bfloat16)
    hidden_grad = jnp.dot(logit_grad, student_head, preferred_element_type=jnp.float32)
    head_grad = jnp.dot(logit_grad.T, student_hidden, preferred_element_type=jnp.float32).astype(jnp.bfloat16)
    return loss, hidden_grad, head_grad
```

```python
import jax
import jax.numpy as jnp
from jax import lax
from jax.sharding import Mesh, PartitionSpec as P

BF = jnp.bfloat16
F32 = jnp.float32
Z, Y, X = 8, 8, 4
TOK = 30
PAD = 32


def exchange(v, axes):
    return lax.all_to_all(v, axes, 0, 0, tiled=True)


def spread(v, axes, n):
    return exchange(jnp.broadcast_to(v[None], (n,) + v.shape), axes)


def swap(v):
    return lax.ppermute(v, "core", [(0, 1), (1, 0)])


def merge(parts):
    m = jnp.max(parts[:, 0:2], axis=0)
    w = jnp.exp(parts[:, 0:2] - m)
    total = jnp.sum(w * parts[:, 2:4], axis=0)
    cross = jnp.sum(w[:, 0:1] * parts[:, 4:5], axis=0)
    return jnp.concatenate([m, total, cross, jnp.zeros((3, m.shape[1]), F32)], axis=0)


def local(student_hidden, teacher_hidden, student_head, teacher_head):
    other_s = swap(student_head)
    other_t = swap(teacher_head)
    fs, ft = student_hidden.shape[1], teacher_hidden.shape[1]
    half = PAD // 2

    sp = jnp.pad(student_hidden, ((0, PAD - TOK), (0, 0)))
    tp = jnp.pad(teacher_hidden, ((0, PAD - TOK), (0, 0)))
    message = jnp.concatenate([tp, jnp.concatenate([sp[:half], sp[half:]], axis=1)], axis=0)
    near = spread(message, ("z", "y"), Z * Y).reshape(Z, Y, PAD + half, ft)
    near_t = near[:, :, :PAD].transpose(0, 2, 1, 3).reshape(Z * PAD, Y * ft)
    near_s = near[:, :, PAD:].reshape(Z, Y, half, 2, fs).transpose(0, 3, 2, 1, 4).reshape(Z * PAD, Y * fs)
    wide = spread(jnp.concatenate([near_t, near_s], axis=1), "x", X)
    full_t = wide[:, :, : Y * ft].reshape(X, Z * PAD, Y, ft).transpose(1, 2, 0, 3).reshape(Z * PAD, X * Y * ft)
    full_s = wide[:, :, Y * ft :].reshape(X, Z * PAD, Y, fs).transpose(1, 2, 0, 3).reshape(Z * PAD, X * Y * fs)

    nt = (((1,), (1,)), ((), ()))
    heads = ((student_head, teacher_head), (other_s, other_t))
    logits = [
        (
            lax.dot_general(hs, full_s, nt, preferred_element_type=F32),
            lax.dot_general(ht, full_t, nt, preferred_element_type=F32),
        )
        for hs, ht in heads
    ]
    stats = []
    for ls, lt in logits:
        mt = jnp.max(lt, axis=0)
        ms = jnp.max(ls, axis=0)
        et = jnp.exp(lt - mt)
        zero = jnp.zeros_like(mt)
        stats.append(
            jnp.stack(
                [
                    mt,
                    ms,
                    jnp.sum(et, axis=0),
                    jnp.sum(jnp.exp(ls - ms), axis=0),
                    jnp.sum(et * (lt - ls), axis=0),
                    zero,
                    zero,
                    zero,
                ]
            )
        )
    mine = merge(jnp.stack(stats))
    plane = merge(spread(mine, ("y", "x"), Y * X))
    whole = merge(spread(plane, "z", Z))
    lse_t = whole[0] + jnp.log(whole[2])
    lse_s = whole[1] + jnp.log(whole[3])
    kl = whole[4] / whole[2] - lse_t + lse_s
    real = (lax.iota(jnp.int32, Z * PAD) % PAD) < TOK
    part = jnp.sum(jnp.where(real, kl, 0.0))
    loss = (part + swap(part[None])[0]) / (2 * Z * TOK)

    grads = [(jnp.exp(ls - lse_s) - jnp.exp(lt - lse_t)).astype(BF) for ls, lt in logits]
    sent = jnp.dot(grads[1], full_s, preferred_element_type=F32).astype(BF)
    arrived = swap(sent)
    tn = (((0,), (0,)), ((), ()))
    terms = lax.dot_general(grads[0], student_head, tn, preferred_element_type=F32) + lax.dot_general(
        grads[1], other_s, tn, preferred_element_type=F32
    )
    by_x = terms.reshape(Z * PAD, Y, X, fs).transpose(2, 0, 1, 3).reshape(X, Z * PAD, Y * fs).astype(BF)
    row = jnp.sum(exchange(by_x, "x").astype(F32), axis=0)
    by_zy = (
        row.reshape(Z, 2, half, Y, fs).transpose(0, 3, 2, 1, 4).reshape(Z * Y, half, 2 * fs).astype(BF)
    )
    mine_h = jnp.sum(exchange(by_zy, ("z", "y")).astype(F32), axis=0)
    hidden_grad = jnp.concatenate([mine_h[:, :fs], mine_h[:, fs:]], axis=0)[:TOK]
    kept = jnp.dot(grads[0], full_s, preferred_element_type=F32)
    head_grad = (kept + arrived.astype(F32)).astype(BF)
    return (loss, hidden_grad, head_grad)


def solution(mesh):
    fine = Mesh(mesh.devices.reshape(Z, 2, Y, X), ("z", "core", "y", "x"))
    rows, cols = ("z", "core"), ("y", "x")
    return jax.shard_map(
        local,
        mesh=fine,
        in_specs=(P(rows, cols), P(rows, cols), P(rows + cols, None), P(rows + cols, None)),
        out_specs=(P(), P(rows, cols), P(rows + cols, None)),
        check_vma=False,
    )
```

```python
import functools

import jax
import jax.numpy as jnp
from jax import lax
from jax.experimental import pallas as pl
from jax.experimental.pallas import tpu as pltpu
from jax.sharding import Mesh, PartitionSpec as P

BF = jnp.bfloat16
F32 = jnp.float32
Z, Y, X = 8, 8, 4
YP = 2
YQ = Y // YP
TOK, PAD = 30, 32
HALF = PAD // 2
SIDE = Z * HALF
ALL = 2 * SIDE
FS, FT = 64, 128
HY = Y // 2
PART = HY * (FT + FS)
D_S, D_T = X * Y * FS, X * Y * FT
NT = (((1,), (1,)), ((), ()))


def call(kernel, out, *args, scratch=(), mib=24, flops=0, scalars=0, anywhere=0, cheap=False):
    specs = [pl.BlockSpec(memory_space=pltpu.SMEM)] * scalars
    specs += [pl.BlockSpec(memory_space=pltpu.VMEM)] * (len(args) - scalars - anywhere)
    specs += [pl.BlockSpec(memory_space=pl.ANY)] * anywhere
    outs = jax.tree.map(lambda o: pl.BlockSpec(memory_space=pltpu.VMEM), out)
    size = sum(a.size * a.dtype.itemsize for a in args) + sum(
        o.size * o.dtype.itemsize for o in jax.tree.leaves(out)
    )
    return pl.pallas_call(
        kernel,
        out_shape=out,
        in_specs=specs,
        out_specs=outs,
        scratch_shapes=scratch,
        compiler_params=pltpu.CompilerParams(vmem_limit_bytes=mib << 20),
        cost_estimate=pl.CostEstimate(flops=flops, bytes_accessed=0 if cheap else size, transcendentals=0),
    )(*args)


def array(shape, dtype):
    return jax.ShapeDtypeStruct(shape, dtype)


def message_kernel(s_any, t_any, o_ref, s_in, t_in, s_pad, t_pad, sems):
    copies = [
        pltpu.make_async_copy(s_any, s_in, sems.at[0]),
        pltpu.make_async_copy(t_any, t_in, sems.at[1]),
    ]
    for c in copies:
        c.start()
    s_pad[...] = jnp.zeros_like(s_pad)
    t_pad[...] = jnp.zeros_like(t_pad)
    for c in copies:
        c.wait()
    s_pad[0:TOK, :] = s_in[...].astype(F32)
    t_pad[0:TOK, :] = t_in[...].astype(F32)
    s = jnp.concatenate([s_pad[0:HALF, :], s_pad[HALF:PAD, :]], axis=1).astype(BF)
    both = jnp.concatenate([t_pad[...].astype(BF), s], axis=0)
    for i in range(Z * Y):
        o_ref[i] = both


def block_kernel(g_ref, lo_ref, hi_ref):
    for y in range(Y):
        o_ref = lo_ref if y < HY else hi_ref
        row = (y % HY) * FT
        for h in range(2):
            t = g_ref[:, y, h * HALF : (h + 1) * HALF, :].reshape(SIDE, FT)
            o_ref[row : row + FT, h * SIDE : (h + 1) * SIDE] = t.T
        s = g_ref[:, y, PAD : PAD + HALF, :].reshape(SIDE, 2 * FS).T
        row = HY * FT + (y % HY) * FS
        for h in range(2):
            o_ref[row : row + FS, h * SIDE : (h + 1) * SIDE] = s[h * FS : (h + 1) * FS]


def merged(parts):
    n = parts.shape[0]
    m = parts[0, 0:2]
    for i in range(1, n):
        m = jnp.maximum(m, parts[i, 0:2])
    total = jnp.zeros_like(m)
    cross = jnp.zeros((1, m.shape[1]), F32)
    for i in range(n):
        w = jnp.exp(parts[i, 0:2] - m)
        total = total + w * parts[i, 2:4]
        cross = cross + w[0:1] * parts[i, 4:5]
    return m, total, cross


def rows_of(m, total, cross):
    return jnp.concatenate([m, total, cross, jnp.zeros((3, m.shape[1]), F32)], axis=0)


def early_kernel(x_ref, *refs):
    s_heads, t_heads = refs[0:2], refs[2:4]
    blocks = refs[4:10]
    ls_ref, lt_ref, far_s, far_t, full_t, full_s, sems = refs[10:]
    xi = x_ref[0]
    far = lax.rem(xi + 2, X)
    parts = []
    for i, step in enumerate((0, 1, 3)):
        x = lax.rem(xi + step, X)
        for y in range(Y):
            ref = blocks[2 * i + y // HY]
            row = (y % HY) * FT
            at = pl.multiple_of((y * X + x) * FT, FT)
            parts.append((ref.at[row : row + FT, :], full_t.at[pl.ds(at, FT), :]))
            row = HY * FT + (y % HY) * FS
            at = pl.multiple_of((y * X + x) * FS, FS)
            parts.append((ref.at[row : row + FS, :], full_s.at[pl.ds(at, FS), :]))
    moves = [pltpu.make_async_copy(src, dst, sems.at[i]) for i, (src, dst) in enumerate(parts)]
    for c in moves:
        c.start()
    parts = []
    for b in range(2):
        for y in range(Y):
            cols = slice(y * FT, (y + 1) * FT)
            at = pl.multiple_of((y * X + far) * FT, FT)
            parts.append((t_heads[b].at[:, pl.ds(at, FT)], far_t.at[b, :, cols]))
            at = pl.multiple_of((y * X + far // 2 * 2) * FS, FT)
            parts.append((s_heads[b].at[:, pl.ds(at, FT)], far_s.at[b, :, cols]))
    first = len(moves)
    later = [pltpu.make_async_copy(src, dst, sems.at[first + i]) for i, (src, dst) in enumerate(parts)]
    for c in later:
        c.start()
    for y in range(Y):
        at = pl.multiple_of((y * X + far) * FT, FT)
        full_t[pl.ds(at, FT), :] = jnp.zeros((FT, ALL), BF)
        at = pl.multiple_of((y * X + far) * FS, FS)
        full_s[pl.ds(at, FS), :] = jnp.zeros((FS, ALL), BF)
    for c in moves:
        c.wait()
    for b in range(2):
        ls_ref[b] = jnp.dot(s_heads[b][...], full_s[...], preferred_element_type=F32)
        lt_ref[b] = jnp.dot(t_heads[b][...], full_t[...], preferred_element_type=F32)
    for c in later:
        c.wait()


def late_kernel(x_ref, lo_ref, hi_ref, far_s, far_t, ls_in, lt_in, ls_ref, lt_ref, stat_ref, rows_s, rows_t):
    odd = lax.rem(x_ref[0], 2)
    rows_s[...] = jnp.zeros_like(rows_s)
    for y in range(Y):
        ref = (lo_ref, hi_ref)[y // HY]
        rows_t[y * FT : (y + 1) * FT, :] = ref[(y % HY) * FT : (y % HY + 1) * FT, :]
        row = HY * FT + (y % HY) * FS
        at = pl.multiple_of(y * FT + odd * FS, FS)
        rows_s[pl.ds(at, FS), :] = ref[row : row + FS, :]
    for b in range(2):
        lt_ref[b] = lt_in[b] + jnp.dot(far_t[b], rows_t[...], preferred_element_type=F32)
        ls_ref[b] = ls_in[b] + jnp.dot(far_s[b], rows_s[...], preferred_element_type=F32)
    mt = jnp.maximum(jnp.max(lt_ref[0], axis=0, keepdims=True), jnp.max(lt_ref[1], axis=0, keepdims=True))
    ms = jnp.maximum(jnp.max(ls_ref[0], axis=0, keepdims=True), jnp.max(ls_ref[1], axis=0, keepdims=True))
    sums = [0.0, 0.0, 0.0]
    for b in range(2):
        lt, ls = lt_ref[b], ls_ref[b]
        et = jnp.exp(lt - mt)
        new = (et, jnp.exp(ls - ms), et * (lt - ls))
        sums = [a + jnp.sum(v, axis=0, keepdims=True) for a, v in zip(sums, new)]
    stat = jnp.concatenate([mt, ms] + sums + [jnp.zeros((3, ALL), F32)], axis=0)
    for i in range(Y * X):
        stat_ref[i] = stat


def fill_kernel(x_ref, *refs):
    blocks, o_ref, sems = refs[0:8], refs[9], refs[10]
    moves = []
    for step in range(X):
        x = lax.rem(x_ref[0] + step, X)
        for y in range(Y):
            ref = blocks[2 * step + y // HY]
            row = HY * FT + (y % HY) * FS
            at = pl.multiple_of((y * X + x) * FS, FS)
            dst = o_ref.at[pl.ds(at, FS), :]
            moves.append(pltpu.make_async_copy(ref.at[row : row + FS, :], dst, sems.at[step * Y + y]))
            moves[-1].start()
    for c in moves:
        c.wait()


def merge_kernel(p_ref, o_ref):
    stat = rows_of(*merged(p_ref))
    for i in range(Z):
        o_ref[i] = stat


def grads_kernel(p_ref, ls_ref, lt_ref, s0_ref, s1_ref, g_ref, by_ypx_ref, kl_ref, terms):
    m, total, cross = merged(p_ref)
    lse = m + jnp.log(total)
    lse_t, lse_s = lse[0:1], lse[1:2]
    kl = cross / total[0:1] - lse_t + lse_s
    lane = lax.broadcasted_iota(jnp.int32, (1, ALL), 1)
    padding = (lane >= SIDE) & ((lane & (HALF - 1)) >= TOK - HALF)
    kl_ref[...] = jnp.broadcast_to(jnp.sum(jnp.where(padding, 0.0, kl), axis=1, keepdims=True), kl_ref.shape)
    for b, head in enumerate((s0_ref, s1_ref)):
        g = (jnp.exp(ls_ref[b] - lse_s) - jnp.exp(lt_ref[b] - lse_t)).astype(BF)
        g_ref[b] = g
        part = lax.dot_general(g, head[...], (((0,), (0,)), ((), ())), preferred_element_type=F32)
        terms[...] = part if b == 0 else terms[...] + part
    for yp in range(YP):
        for x in range(X):
            for q in range(YQ // 2):
                ys = [(2 * q + i) * YP + yp for i in range(2)]
                pair = [terms[:, (y * X + x) * FS : (y * X + x + 1) * FS] for y in ys]
                by_ypx_ref[yp * X + x, :, q * 2 * FS : (q + 1) * 2 * FS] = jnp.concatenate(pair, axis=1).astype(BF)


def thirds(v):
    hi = v.astype(BF)
    mid = (v - hi.astype(F32)).astype(BF)
    return hi, mid, (v - hi.astype(F32) - mid.astype(F32)).astype(BF)


def sent_kernel(g_ref, full_s, kl_ref, o_ref):
    o_ref[:, 0:D_S] = lax.dot_general(g_ref[1], full_s[...], NT, preferred_element_type=F32).astype(BF)
    lane = lax.broadcasted_iota(jnp.int32, (1, 128), 1)
    row = jnp.zeros((1, 128), F32)
    for i, v in enumerate(thirds(kl_ref[0:1, :])):
        row = jnp.where(lane == i, v.astype(F32), row)
    o_ref[:, D_S : D_S + 128] = jnp.broadcast_to(row, (o_ref.shape[0], 128)).astype(BF)


def kept_kernel(g_ref, full_s, kl_ref, arrived, o_ref, loss_ref):
    kept = lax.dot_general(g_ref[0], full_s[...], NT, preferred_element_type=F32)
    o_ref[...] = (kept + arrived[:, 0:D_S].astype(F32)).astype(BF)
    hi, mid, lo = [v.astype(F32) for v in thirds(kl_ref[0:1, 0:1])]
    other = arrived[0:16, D_S : D_S + 128].astype(F32)[0:1]
    there = other[:, 0:1] + other[:, 1:2] + other[:, 2:3]
    loss_ref[...] = (hi + mid + lo + there) / (2 * Z * TOK)


def pack_kernel(r_ref, _, o_ref):
    row = r_ref[0].astype(F32)
    for i in range(1, YP * X):
        row = row + r_ref[i].astype(F32)
    for z in range(Z):
        sides = [row[h * SIDE + z * HALF : h * SIDE + (z + 1) * HALF] for h in range(2)]
        for yq in range(YQ):
            pair = [v[:, yq * FS : (yq + 1) * FS] for v in sides]
            o_ref[z * YQ + yq] = jnp.concatenate(pair, axis=1).astype(BF)


def last_kernel(r_ref, o_ref):
    total = jnp.sum(r_ref[...].astype(F32), axis=0)
    o_ref[0:HALF, :] = total[:, 0:FS]
    o_ref[HALF:TOK, :] = total[0 : TOK - HALF, FS : 2 * FS]


def exchange(v, axes):
    return lax.all_to_all(v, axes, 0, 0, tiled=True)


def swap(v):
    return lax.ppermute(v, "core", [(0, 1), (1, 0)])


def along_x(v, step):
    return lax.ppermute(v, "x", [(i, (i + step) % X) for i in range(X)])


def local(student_hidden, teacher_hidden, student_head, teacher_head):
    rows = student_head.shape[0]
    xi = lax.axis_index("x").reshape(1)
    s_heads = [student_head, swap(student_head)]
    t_heads = [teacher_head, swap(teacher_head)]

    message = call(
        message_kernel,
        array((Z * Y, PAD + HALF, FT), BF),
        student_hidden,
        teacher_hidden,
        anywhere=2,
        mib=60,
        scratch=[
            pltpu.VMEM((TOK, FS), BF),
            pltpu.VMEM((TOK, FT), BF),
            pltpu.VMEM((PAD, FS), F32),
            pltpu.VMEM((PAD, FT), F32),
            pltpu.SemaphoreType.DMA((2,)),
        ],
    )
    near = exchange(message, ("z", "yq", "yp")).reshape(Z, Y, PAD + HALF, FT)
    part = array((PART, ALL), BF)
    own = call(block_kernel, (part, part), near)
    before = [along_x(v, 1) for v in own]
    after = [along_x(v, -1) for v in own]
    far = [along_x(before[0], 1), along_x(after[1], -1)]

    logit = array((2, rows, ALL), F32)
    far_cols = array((2, rows, Y * FT), BF)
    ls, lt, far_s, far_t = call(
        early_kernel,
        (logit, logit, far_cols, far_cols),
        xi,
        *s_heads,
        *t_heads,
        *own,
        *after,
        *before,
        scalars=1,
        anywhere=6,
        mib=16,
        cheap=True,
        scratch=[
            pltpu.VMEM((D_T, ALL), BF),
            pltpu.VMEM((D_S, ALL), BF),
            pltpu.SemaphoreType.DMA((10 * Y,)),
        ],
    )
    ls, lt, stat = call(
        late_kernel,
        (logit, logit, array((Y * X, 8, ALL), F32)),
        xi,
        *far,
        far_s,
        far_t,
        ls,
        lt,
        scalars=1,
        scratch=[pltpu.VMEM((Y * FT, ALL), BF), pltpu.VMEM((Y * FT, ALL), BF)],
        flops=8 * rows * ALL * Y * FT,
    )
    stat = exchange(stat, ("yq", "yp", "x"))
    stat = call(merge_kernel, array((Z, 8, ALL), F32), stat)
    stat = exchange(stat, "z")
    grads, by_ypx, kl = call(
        grads_kernel,
        (array((2, rows, ALL), BF), array((YP * X, ALL, YQ * FS), BF), array((8, 128), F32)),
        stat,
        ls,
        lt,
        *s_heads,
        scratch=[pltpu.VMEM((ALL, D_S), F32)],
        flops=4 * rows * ALL * D_S,
    )
    full_s = call(
        fill_kernel,
        array((D_S, ALL), BF),
        xi,
        *own,
        *after,
        *far,
        *before,
        kl,
        scalars=1,
        anywhere=9,
        scratch=[pltpu.SemaphoreType.DMA((X * Y,))],
    )
    sent = call(sent_kernel, array((rows, D_S + 128), BF), grads, full_s, kl, flops=2 * rows * ALL * D_S)
    packed = call(
        pack_kernel, array((Z * YQ, HALF, 2 * FS), BF), exchange(by_ypx, ("yp", "x")), sent, anywhere=1
    )
    hidden_grad = call(last_kernel, array((TOK, FS), F32), exchange(packed, ("z", "yq")))
    head_grad, loss = call(
        kept_kernel,
        (array((rows, D_S), BF), array((1, 1), F32)),
        grads,
        full_s,
        kl,
        swap(sent),
        flops=2 * rows * ALL * D_S,
    )
    return (loss.reshape(()), hidden_grad, head_grad)


def solution(mesh):
    fine = Mesh(mesh.devices.reshape(Z, 2, YQ, YP, X), ("z", "core", "yq", "yp", "x"))
    rows, cols = ("z", "core"), ("yq", "yp", "x")
    return jax.shard_map(
        local,
        mesh=fine,
        in_specs=(P(rows, cols), P(rows, cols), P(rows + cols, None), P(rows + cols, None)),
        out_specs=(P(), P(rows, cols), P(rows + cols, None)),
        check_vma=False,
    )
```

```python
import functools

import jax
import jax.numpy as jnp
from jax import lax
from jax.experimental import pallas as pl
from jax.experimental.pallas import tpu as pltpu
from jax.sharding import Mesh, PartitionSpec as P

BF = jnp.bfloat16
F32 = jnp.float32
Z, Y, X = 8, 8, 4
YP = 2
YQ = Y // YP
TOK, PAD = 30, 32
HALF = PAD // 2
SIDE = Z * HALF
ALL = 2 * SIDE
FS, FT = 64, 128
HY = Y // 2
PART = HY * (FT + FS)
D_S, D_T = X * Y * FS, X * Y * FT
NT = (((1,), (1,)), ((), ()))


def call(kernel, out, *args, scratch=(), mib=24, flops=0, scalars=0, anywhere=0, cheap=False):
    specs = [pl.BlockSpec(memory_space=pltpu.SMEM)] * scalars
    specs += [pl.BlockSpec(memory_space=pltpu.VMEM)] * (len(args) - scalars - anywhere)
    specs += [pl.BlockSpec(memory_space=pl.ANY)] * anywhere
    outs = jax.tree.map(lambda o: pl.BlockSpec(memory_space=pltpu.VMEM), out)
    size = sum(a.size * a.dtype.itemsize for a in args) + sum(
        o.size * o.dtype.itemsize for o in jax.tree.leaves(out)
    )
    return pl.pallas_call(
        kernel,
        out_shape=out,
        in_specs=specs,
        out_specs=outs,
        scratch_shapes=scratch,
        compiler_params=pltpu.CompilerParams(vmem_limit_bytes=mib << 20),
        cost_estimate=pl.CostEstimate(flops=flops, bytes_accessed=0 if cheap else size, transcendentals=0),
    )(*args)


def array(shape, dtype):
    return jax.ShapeDtypeStruct(shape, dtype)


def message_kernel(s_any, t_any, o_ref, s_in, t_in, s_pad, t_pad, sems):
    copies = [
        pltpu.make_async_copy(s_any, s_in, sems.at[0]),
        pltpu.make_async_copy(t_any, t_in, sems.at[1]),
    ]
    for c in copies:
        c.start()
    s_pad[...] = jnp.zeros_like(s_pad)
    t_pad[...] = jnp.zeros_like(t_pad)
    for c in copies:
        c.wait()
    s_pad[0:TOK, :] = s_in[...].astype(F32)
    t_pad[0:TOK, :] = t_in[...].astype(F32)
    s = jnp.concatenate([s_pad[0:HALF, :], s_pad[HALF:PAD, :]], axis=1).astype(BF)
    both = jnp.concatenate([t_pad[...].astype(BF), s], axis=0)
    for i in range(Z * Y):
        o_ref[i] = both


def block_kernel(g_ref, lo_ref, hi_ref):
    for y in range(Y):
        o_ref = lo_ref if y < HY else hi_ref
        row = (y % HY) * FT
        for h in range(2):
            t = g_ref[:, y, h * HALF : (h + 1) * HALF, :].reshape(SIDE, FT)
            o_ref[row : row + FT, h * SIDE : (h + 1) * SIDE] = t.T
        s = g_ref[:, y, PAD : PAD + HALF, :].reshape(SIDE, 2 * FS).T
        row = HY * FT + (y % HY) * FS
        for h in range(2):
            o_ref[row : row + FS, h * SIDE : (h + 1) * SIDE] = s[h * FS : (h + 1) * FS]


def merged(parts):
    n = parts.shape[0]
    m = parts[0, 0:2]
    for i in range(1, n):
        m = jnp.maximum(m, parts[i, 0:2])
    total = jnp.zeros_like(m)
    cross = jnp.zeros((1, m.shape[1]), F32)
    for i in range(n):
        w = jnp.exp(parts[i, 0:2] - m)
        total = total + w * parts[i, 2:4]
        cross = cross + w[0:1] * parts[i, 4:5]
    return m, total, cross


def rows_of(m, total, cross):
    return jnp.concatenate([m, total, cross, jnp.zeros((3, m.shape[1]), F32)], axis=0)


def early_kernel(x_ref, *refs):
    s_heads, t_heads, blocks = refs[0:2], refs[2:4], refs[4:10]
    ls_ref, lt_ref, far_s, far_t, full_t, full_s, sems = refs[10:]
    xi = x_ref[0]
    far = lax.rem(xi + 2, X)
    for i, step in enumerate((0, 1, 3)):
        x = lax.rem(xi + step, X)
        for y in range(Y):
            ref = blocks[2 * i + y // HY]
            row = HY * FT + (y % HY) * FS
            at = pl.multiple_of((y * X + x) * FS, FS)
            pltpu.make_async_copy(ref.at[row : row + FS, :], full_s.at[pl.ds(at, FS), :], sems.at[0]).start()
            row = (y % HY) * FT
            at = pl.multiple_of((y * X + x) * FT, FT)
            pltpu.make_async_copy(ref.at[row : row + FT, :], full_t.at[pl.ds(at, FT), :], sems.at[1]).start()
    parts = []
    for b in range(2):
        for y in range(Y):
            cols = slice(y * FT, (y + 1) * FT)
            at = pl.multiple_of((y * X + far) * FT, FT)
            parts.append((t_heads[b].at[:, pl.ds(at, FT)], far_t.at[b, :, cols]))
            at = pl.multiple_of((y * X + far // 2 * 2) * FS, FT)
            parts.append((s_heads[b].at[:, pl.ds(at, FT)], far_s.at[b, :, cols]))
    later = [pltpu.make_async_copy(src, dst, sems.at[2 + i]) for i, (src, dst) in enumerate(parts)]
    for c in later:
        c.start()
    for y in range(Y):
        at = pl.multiple_of((y * X + far) * FT, FT)
        full_t[pl.ds(at, FT), :] = jnp.zeros((FT, ALL), BF)
        at = pl.multiple_of((y * X + far) * FS, FS)
        full_s[pl.ds(at, FS), :] = jnp.zeros((FS, ALL), BF)
    arrived = full_s.at[0 : D_S // X * 3, :]
    pltpu.make_async_copy(arrived, arrived, sems.at[0]).wait()
    for b in range(2):
        ls_ref[b] = jnp.dot(s_heads[b][...], full_s[...], preferred_element_type=F32)
    arrived = full_t.at[0 : D_T // X * 3, :]
    pltpu.make_async_copy(arrived, arrived, sems.at[1]).wait()
    for b in range(2):
        lt_ref[b] = jnp.dot(t_heads[b][...], full_t[...], preferred_element_type=F32)
    for c in later:
        c.wait()


def late_kernel(x_ref, lo_ref, hi_ref, far_s, far_t, ls_in, lt_in, ls_ref, lt_ref, stat_ref, rows_s, rows_t):
    odd = lax.rem(x_ref[0], 2)
    rows_s[...] = jnp.zeros_like(rows_s)
    for y in range(Y):
        ref = (lo_ref, hi_ref)[y // HY]
        rows_t[y * FT : (y + 1) * FT, :] = ref[(y % HY) * FT : (y % HY + 1) * FT, :]
        row = HY * FT + (y % HY) * FS
        at = pl.multiple_of(y * FT + odd * FS, FS)
        rows_s[pl.ds(at, FS), :] = ref[row : row + FS, :]
    for b in range(2):
        lt_ref[b] = lt_in[b] + jnp.dot(far_t[b], rows_t[...], preferred_element_type=F32)
        ls_ref[b] = ls_in[b] + jnp.dot(far_s[b], rows_s[...], preferred_element_type=F32)
    mt = jnp.maximum(jnp.max(lt_ref[0], axis=0, keepdims=True), jnp.max(lt_ref[1], axis=0, keepdims=True))
    ms = jnp.maximum(jnp.max(ls_ref[0], axis=0, keepdims=True), jnp.max(ls_ref[1], axis=0, keepdims=True))
    sums = [0.0, 0.0, 0.0]
    for b in range(2):
        lt, ls = lt_ref[b], ls_ref[b]
        et = jnp.exp(lt - mt)
        new = (et, jnp.exp(ls - ms), et * (lt - ls))
        sums = [a + jnp.sum(v, axis=0, keepdims=True) for a, v in zip(sums, new)]
    stat = jnp.concatenate([mt, ms] + sums + [jnp.zeros((3, ALL), F32)], axis=0)
    for i in range(Y * X):
        stat_ref[i] = stat


def fill_kernel(x_ref, *refs):
    blocks, o_ref, sem = refs[0:8], refs[9], refs[10]
    for step in range(X):
        x = lax.rem(x_ref[0] + step, X)
        for y in range(Y):
            ref = blocks[2 * step + y // HY]
            row = HY * FT + (y % HY) * FS
            at = pl.multiple_of((y * X + x) * FS, FS)
            pltpu.make_async_copy(ref.at[row : row + FS, :], o_ref.at[pl.ds(at, FS), :], sem).start()
    pltpu.make_async_copy(o_ref, o_ref, sem).wait()


def merge_kernel(p_ref, o_ref):
    stat = rows_of(*merged(p_ref))
    for i in range(Z):
        o_ref[i] = stat


def grads_kernel(p_ref, ls_ref, lt_ref, s0_ref, s1_ref, g_ref, by_ypx_ref, kl_ref, terms):
    m, total, cross = merged(p_ref)
    lse = m + jnp.log(total)
    lse_t, lse_s = lse[0:1], lse[1:2]
    kl = cross / total[0:1] - lse_t + lse_s
    lane = lax.broadcasted_iota(jnp.int32, (1, ALL), 1)
    padding = (lane >= SIDE) & ((lane & (HALF - 1)) >= TOK - HALF)
    kl_ref[...] = jnp.broadcast_to(jnp.sum(jnp.where(padding, 0.0, kl), axis=1, keepdims=True), kl_ref.shape)
    for b, head in enumerate((s0_ref, s1_ref)):
        g = (jnp.exp(ls_ref[b] - lse_s) - jnp.exp(lt_ref[b] - lse_t)).astype(BF)
        g_ref[b] = g
        part = lax.dot_general(g, head[...], (((0,), (0,)), ((), ())), preferred_element_type=F32)
        terms[...] = part if b == 0 else terms[...] + part
    for yp in range(YP):
        for x in range(X):
            for q in range(YQ // 2):
                ys = [(2 * q + i) * YP + yp for i in range(2)]
                pair = [terms[:, (y * X + x) * FS : (y * X + x + 1) * FS] for y in ys]
                by_ypx_ref[yp * X + x, :, q * 2 * FS : (q + 1) * 2 * FS] = jnp.concatenate(pair, axis=1).astype(BF)


def thirds(v):
    hi = v.astype(BF)
    mid = (v - hi.astype(F32)).astype(BF)
    return hi, mid, (v - hi.astype(F32) - mid.astype(F32)).astype(BF)


def sent_kernel(g_ref, full_s, kl_ref, o_ref):
    o_ref[:, 0:D_S] = lax.dot_general(g_ref[1], full_s[...], NT, preferred_element_type=F32).astype(BF)
    lane = lax.broadcasted_iota(jnp.int32, (1, 128), 1)
    row = jnp.zeros((1, 128), F32)
    for i, v in enumerate(thirds(kl_ref[0:1, :])):
        row = jnp.where(lane == i, v.astype(F32), row)
    o_ref[:, D_S : D_S + 128] = jnp.broadcast_to(row, (o_ref.shape[0], 128)).astype(BF)


def kept_kernel(g_ref, full_s, kl_ref, arrived, o_ref, loss_ref):
    kept = lax.dot_general(g_ref[0], full_s[...], NT, preferred_element_type=F32)
    o_ref[...] = (kept + arrived[:, 0:D_S].astype(F32)).astype(BF)
    hi, mid, lo = [v.astype(F32) for v in thirds(kl_ref[0:1, 0:1])]
    other = arrived[0:16, D_S : D_S + 128].astype(F32)[0:1]
    there = other[:, 0:1] + other[:, 1:2] + other[:, 2:3]
    loss_ref[...] = (hi + mid + lo + there) / (2 * Z * TOK)


def pack_kernel(r_ref, _, o_ref):
    row = r_ref[0].astype(F32)
    for i in range(1, YP * X):
        row = row + r_ref[i].astype(F32)
    for z in range(Z):
        sides = [row[h * SIDE + z * HALF : h * SIDE + (z + 1) * HALF] for h in range(2)]
        for yq in range(YQ):
            pair = [v[:, yq * FS : (yq + 1) * FS] for v in sides]
            o_ref[z * YQ + yq] = jnp.concatenate(pair, axis=1).astype(BF)


def last_kernel(r_ref, o_ref):
    total = jnp.sum(r_ref[...].astype(F32), axis=0)
    o_ref[0:HALF, :] = total[:, 0:FS]
    o_ref[HALF:TOK, :] = total[0 : TOK - HALF, FS : 2 * FS]


def exchange(v, axes):
    return lax.all_to_all(v, axes, 0, 0, tiled=True)


def swap(v):
    return lax.ppermute(v, "core", [(0, 1), (1, 0)])


def along_x(v, step):
    return lax.ppermute(v, "x", [(i, (i + step) % X) for i in range(X)])


def local(student_hidden, teacher_hidden, student_head, teacher_head):
    rows = student_head.shape[0]
    xi = lax.axis_index("x").reshape(1)
    s_heads = [student_head, swap(student_head)]
    t_heads = [teacher_head, swap(teacher_head)]

    message = call(
        message_kernel,
        array((Z * Y, PAD + HALF, FT), BF),
        student_hidden,
        teacher_hidden,
        anywhere=2,
        mib=60,
        scratch=[
            pltpu.VMEM((TOK, FS), BF),
            pltpu.VMEM((TOK, FT), BF),
            pltpu.VMEM((PAD, FS), F32),
            pltpu.VMEM((PAD, FT), F32),
            pltpu.SemaphoreType.DMA((2,)),
        ],
    )
    near = exchange(message, ("z", "yq", "yp")).reshape(Z, Y, PAD + HALF, FT)
    part = array((PART, ALL), BF)
    own = call(block_kernel, (part, part), near)
    before = [along_x(v, 1) for v in own]
    after = [along_x(v, -1) for v in own]
    far = [along_x(before[0], 1), along_x(after[1], -1)]

    logit = array((2, rows, ALL), F32)
    far_cols = array((2, rows, Y * FT), BF)
    ls, lt, far_s, far_t = call(
        early_kernel,
        (logit, logit, far_cols, far_cols),
        xi,
        *s_heads,
        *t_heads,
        *own,
        *after,
        *before,
        scalars=1,
        anywhere=6,
        mib=16,
        cheap=True,
        scratch=[
            pltpu.VMEM((D_T, ALL), BF),
            pltpu.VMEM((D_S, ALL), BF),
            pltpu.SemaphoreType.DMA((2 + 4 * Y,)),
        ],
    )
    ls, lt, stat = call(
        late_kernel,
        (logit, logit, array((Y * X, 8, ALL), F32)),
        xi,
        *far,
        far_s,
        far_t,
        ls,
        lt,
        scalars=1,
        scratch=[pltpu.VMEM((Y * FT, ALL), BF), pltpu.VMEM((Y * FT, ALL), BF)],
        flops=8 * rows * ALL * Y * FT,
    )
    stat = exchange(stat, ("yq", "yp", "x"))
    stat = call(merge_kernel, array((Z, 8, ALL), F32), stat)
    stat = exchange(stat, "z")
    grads, by_ypx, kl = call(
        grads_kernel,
        (array((2, rows, ALL), BF), array((YP * X, ALL, YQ * FS), BF), array((8, 128), F32)),
        stat,
        ls,
        lt,
        *s_heads,
        scratch=[pltpu.VMEM((ALL, D_S), F32)],
        flops=4 * rows * ALL * D_S,
    )
    full_s = call(
        fill_kernel,
        array((D_S, ALL), BF),
        xi,
        *own,
        *after,
        *far,
        *before,
        kl,
        scalars=1,
        anywhere=9,
        scratch=[pltpu.SemaphoreType.DMA],
    )
    sent = call(sent_kernel, array((rows, D_S + 128), BF), grads, full_s, kl, flops=2 * rows * ALL * D_S)
    packed = call(
        pack_kernel, array((Z * YQ, HALF, 2 * FS), BF), exchange(by_ypx, ("yp", "x")), sent, anywhere=1
    )
    hidden_grad = call(last_kernel, array((TOK, FS), F32), exchange(packed, ("z", "yq")))
    head_grad, loss = call(
        kept_kernel,
        (array((rows, D_S), BF), array((1, 1), F32)),
        grads,
        full_s,
        kl,
        swap(sent),
        flops=2 * rows * ALL * D_S,
    )
    return (loss.reshape(()), hidden_grad, head_grad)


def solution(mesh):
    fine = Mesh(mesh.devices.reshape(Z, 2, YQ, YP, X), ("z", "core", "yq", "yp", "x"))
    rows, cols = ("z", "core"), ("yq", "yp", "x")
    return jax.shard_map(
        local,
        mesh=fine,
        in_specs=(P(rows, cols), P(rows, cols), P(rows + cols, None), P(rows + cols, None)),
        out_specs=(P(), P(rows, cols), P(rows + cols, None)),
        check_vma=False,
    )
```

```python
import functools

import jax
import jax.numpy as jnp
from jax import lax
from jax.experimental import pallas as pl
from jax.experimental.pallas import tpu as pltpu
from jax.sharding import Mesh, PartitionSpec as P

BF = jnp.bfloat16
F32 = jnp.float32
Z, Y, X = 8, 8, 4
YP = 2
YQ = Y // YP
TOK, PAD = 30, 32
HALF = PAD // 2
SIDE = Z * HALF
ALL = 2 * SIDE
FS, FT = 64, 128
HY = Y // 2
PART = HY * (FT + FS)
D_S, D_T = X * Y * FS, X * Y * FT
NT = (((1,), (1,)), ((), ()))


def call(kernel, out, *args, scratch=(), mib=24, flops=0, scalars=0, anywhere=0, cheap=False):
    specs = [pl.BlockSpec(memory_space=pltpu.SMEM)] * scalars
    specs += [pl.BlockSpec(memory_space=pltpu.VMEM)] * (len(args) - scalars - anywhere)
    specs += [pl.BlockSpec(memory_space=pl.ANY)] * anywhere
    outs = jax.tree.map(lambda o: pl.BlockSpec(memory_space=pltpu.VMEM), out)
    size = sum(a.size * a.dtype.itemsize for a in args) + sum(
        o.size * o.dtype.itemsize for o in jax.tree.leaves(out)
    )
    return pl.pallas_call(
        kernel,
        out_shape=out,
        in_specs=specs,
        out_specs=outs,
        scratch_shapes=scratch,
        compiler_params=pltpu.CompilerParams(vmem_limit_bytes=mib << 20),
        cost_estimate=pl.CostEstimate(flops=flops, bytes_accessed=0 if cheap else size, transcendentals=0),
    )(*args)


def array(shape, dtype):
    return jax.ShapeDtypeStruct(shape, dtype)


def message_kernel(s_any, t_any, o_ref, s_in, t_in, s_pad, t_pad, sems):
    copies = [
        pltpu.make_async_copy(s_any, s_in, sems.at[0]),
        pltpu.make_async_copy(t_any, t_in, sems.at[1]),
    ]
    for c in copies:
        c.start()
    s_pad[...] = jnp.zeros_like(s_pad)
    t_pad[...] = jnp.zeros_like(t_pad)
    for c in copies:
        c.wait()
    s_pad[0:TOK, :] = s_in[...].astype(F32)
    t_pad[0:TOK, :] = t_in[...].astype(F32)
    s = jnp.concatenate([s_pad[0:HALF, :], s_pad[HALF:PAD, :]], axis=1).astype(BF)
    both = jnp.concatenate([t_pad[...].astype(BF), s], axis=0)
    for i in range(Z * Y):
        o_ref[i] = both


def block_kernel(g_ref, lo_ref, hi_ref):
    for y in range(Y):
        o_ref = lo_ref if y < HY else hi_ref
        row = (y % HY) * FT
        for h in range(2):
            t = g_ref[:, y, h * HALF : (h + 1) * HALF, :].reshape(SIDE, FT)
            o_ref[row : row + FT, h * SIDE : (h + 1) * SIDE] = t.T
        s = g_ref[:, y, PAD : PAD + HALF, :].reshape(SIDE, 2 * FS).T
        row = HY * FT + (y % HY) * FS
        for h in range(2):
            o_ref[row : row + FS, h * SIDE : (h + 1) * SIDE] = s[h * FS : (h + 1) * FS]


def merged(parts):
    n = parts.shape[0]
    m = parts[0, 0:4]
    for i in range(1, n):
        m = jnp.maximum(m, parts[i, 0:4])
    total = jnp.zeros_like(m)
    cross = jnp.zeros((2, m.shape[1]), F32)
    for i in range(n):
        w = jnp.exp(parts[i, 0:4] - m)
        total = total + w
        cross = cross + w[0:2] * parts[i, 4:6]
    return m + jnp.log(total), cross / total[0:2]


def rows_of(lse, cross):
    return jnp.concatenate([lse, cross, jnp.zeros((2, lse.shape[1]), F32)], axis=0)


def halves(v):
    return [v[:, 0:SIDE], v[:, SIDE:ALL]]


def early_kernel(x_ref, *refs):
    s_heads, t_heads, blocks = refs[0:2], refs[2:4], refs[4:10]
    ls_ref, lt_ref, far_s, far_t, full_t, full_s, sems = refs[10:]
    xi = x_ref[0]
    far = lax.rem(xi + 2, X)
    for i, step in enumerate((0, 1, 3)):
        x = lax.rem(xi + step, X)
        for y in range(Y):
            ref = blocks[2 * i + y // HY]
            row = HY * FT + (y % HY) * FS
            at = pl.multiple_of((y * X + x) * FS, FS)
            pltpu.make_async_copy(ref.at[row : row + FS, :], full_s.at[pl.ds(at, FS), :], sems.at[0]).start()
            row = (y % HY) * FT
            at = pl.multiple_of((y * X + x) * FT, FT)
            pltpu.make_async_copy(ref.at[row : row + FT, :], full_t.at[pl.ds(at, FT), :], sems.at[1]).start()
    parts = []
    for b in range(2):
        for y in range(Y):
            cols = slice(y * FT, (y + 1) * FT)
            at = pl.multiple_of((y * X + far) * FT, FT)
            parts.append((t_heads[b].at[:, pl.ds(at, FT)], far_t.at[b, :, cols]))
            at = pl.multiple_of((y * X + far // 2 * 2) * FS, FT)
            parts.append((s_heads[b].at[:, pl.ds(at, FT)], far_s.at[b, :, cols]))
    later = [pltpu.make_async_copy(src, dst, sems.at[2 + i]) for i, (src, dst) in enumerate(parts)]
    for c in later:
        c.start()
    for y in range(Y):
        at = pl.multiple_of((y * X + far) * FT, FT)
        full_t[pl.ds(at, FT), :] = jnp.zeros((FT, ALL), BF)
        at = pl.multiple_of((y * X + far) * FS, FS)
        full_s[pl.ds(at, FS), :] = jnp.zeros((FS, ALL), BF)
    arrived = full_s.at[0 : D_S // X * 3, :]
    pltpu.make_async_copy(arrived, arrived, sems.at[0]).wait()
    for b in range(2):
        ls_ref[b] = jnp.dot(s_heads[b][...], full_s[...], preferred_element_type=F32)
    arrived = full_t.at[0 : D_T // X * 3, :]
    pltpu.make_async_copy(arrived, arrived, sems.at[1]).wait()
    for b in range(2):
        lt_ref[b] = jnp.dot(t_heads[b][...], full_t[...], preferred_element_type=F32)
    for c in later:
        c.wait()


def late_kernel(x_ref, lo_ref, hi_ref, far_s, far_t, ls_in, lt_in, ls_ref, lt_ref, stat_ref, rows_s, rows_t):
    odd = lax.rem(x_ref[0], 2)
    rows_s[...] = jnp.zeros_like(rows_s)
    for y in range(Y):
        ref = (lo_ref, hi_ref)[y // HY]
        rows_t[y * FT : (y + 1) * FT, :] = ref[(y % HY) * FT : (y % HY + 1) * FT, :]
        row = HY * FT + (y % HY) * FS
        at = pl.multiple_of(y * FT + odd * FS, FS)
        rows_s[pl.ds(at, FS), :] = ref[row : row + FS, :]
    for b in range(2):
        lt_ref[b] = lt_in[b] + jnp.dot(far_t[b], rows_t[...], preferred_element_type=F32)
        ls_ref[b] = ls_in[b] + jnp.dot(far_s[b], rows_s[...], preferred_element_type=F32)
    mt = jnp.maximum(jnp.max(lt_ref[0], axis=0, keepdims=True), jnp.max(lt_ref[1], axis=0, keepdims=True))
    ms = jnp.maximum(jnp.max(ls_ref[0], axis=0, keepdims=True), jnp.max(ls_ref[1], axis=0, keepdims=True))
    sums = [0.0, 0.0, 0.0]
    for b in range(2):
        lt, ls = lt_ref[b], ls_ref[b]
        et = jnp.exp(lt - mt)
        new = (et, jnp.exp(ls - ms), et * (lt - ls))
        sums = [a + jnp.sum(v, axis=0, keepdims=True) for a, v in zip(sums, new)]
    lse = halves(mt + jnp.log(sums[0])) + halves(ms + jnp.log(sums[1]))
    stat = rows_of(jnp.concatenate(lse, axis=0), jnp.concatenate(halves(sums[2] / sums[0]), axis=0))
    for i in range(Y * X):
        stat_ref[i] = stat


def fill_kernel(x_ref, *refs):
    blocks, o_ref, sem = refs[0:8], refs[9], refs[10]
    for step in range(X):
        x = lax.rem(x_ref[0] + step, X)
        for y in range(Y):
            ref = blocks[2 * step + y // HY]
            row = HY * FT + (y % HY) * FS
            at = pl.multiple_of((y * X + x) * FS, FS)
            pltpu.make_async_copy(ref.at[row : row + FS, :], o_ref.at[pl.ds(at, FS), :], sem).start()
    pltpu.make_async_copy(o_ref, o_ref, sem).wait()


def merge_kernel(p_ref, o_ref):
    stat = rows_of(*merged(p_ref))
    for i in range(Z):
        o_ref[i] = stat


def grads_kernel(p_ref, ls_ref, lt_ref, s0_ref, s1_ref, g_ref, by_ypx_ref, kl_ref, terms):
    lse, cross = merged(p_ref)
    lse_t = jnp.concatenate([lse[0:1], lse[1:2]], axis=1)
    lse_s = jnp.concatenate([lse[2:3], lse[3:4]], axis=1)
    kl = jnp.concatenate([cross[0:1], cross[1:2]], axis=1) - lse_t + lse_s
    lane = lax.broadcasted_iota(jnp.int32, (1, ALL), 1)
    padding = (lane >= SIDE) & ((lane & (HALF - 1)) >= TOK - HALF)
    kl_ref[...] = jnp.broadcast_to(jnp.sum(jnp.where(padding, 0.0, kl), axis=1, keepdims=True), kl_ref.shape)
    for b, head in enumerate((s0_ref, s1_ref)):
        g = (jnp.exp(ls_ref[b] - lse_s) - jnp.exp(lt_ref[b] - lse_t)).astype(BF)
        g_ref[b] = g
        part = lax.dot_general(g, head[...], (((0,), (0,)), ((), ())), preferred_element_type=F32)
        terms[...] = part if b == 0 else terms[...] + part
    for yp in range(YP):
        for x in range(X):
            for q in range(YQ // 2):
                ys = [(2 * q + i) * YP + yp for i in range(2)]
                pair = [terms[:, (y * X + x) * FS : (y * X + x + 1) * FS] for y in ys]
                by_ypx_ref[yp * X + x, :, q * 2 * FS : (q + 1) * 2 * FS] = jnp.concatenate(pair, axis=1).astype(BF)


def thirds(v):
    hi = v.astype(BF)
    mid = (v - hi.astype(F32)).astype(BF)
    return hi, mid, (v - hi.astype(F32) - mid.astype(F32)).astype(BF)


def sent_kernel(g_ref, full_s, kl_ref, o_ref):
    o_ref[:, 0:D_S] = lax.dot_general(g_ref[1], full_s[...], NT, preferred_element_type=F32).astype(BF)
    lane = lax.broadcasted_iota(jnp.int32, (1, 128), 1)
    row = jnp.zeros((1, 128), F32)
    for i, v in enumerate(thirds(kl_ref[0:1, :])):
        row = jnp.where(lane == i, v.astype(F32), row)
    o_ref[:, D_S : D_S + 128] = jnp.broadcast_to(row, (o_ref.shape[0], 128)).astype(BF)


def kept_kernel(g_ref, full_s, kl_ref, arrived, o_ref, loss_ref):
    kept = lax.dot_general(g_ref[0], full_s[...], NT, preferred_element_type=F32)
    o_ref[...] = (kept + arrived[:, 0:D_S].astype(F32)).astype(BF)
    hi, mid, lo = [v.astype(F32) for v in thirds(kl_ref[0:1, 0:1])]
    other = arrived[0:16, D_S : D_S + 128].astype(F32)[0:1]
    there = other[:, 0:1] + other[:, 1:2] + other[:, 2:3]
    loss_ref[...] = (hi + mid + lo + there) / (2 * Z * TOK)


def pack_kernel(r_ref, _, o_ref):
    row = r_ref[0].astype(F32)
    for i in range(1, YP * X):
        row = row + r_ref[i].astype(F32)
    for z in range(Z):
        sides = [row[h * SIDE + z * HALF : h * SIDE + (z + 1) * HALF] for h in range(2)]
        for yq in range(YQ):
            pair = [v[:, yq * FS : (yq + 1) * FS] for v in sides]
            o_ref[z * YQ + yq] = jnp.concatenate(pair, axis=1).astype(BF)


def last_kernel(r_ref, o_ref):
    total = jnp.sum(r_ref[...].astype(F32), axis=0)
    o_ref[0:HALF, :] = total[:, 0:FS]
    o_ref[HALF:TOK, :] = total[0 : TOK - HALF, FS : 2 * FS]


def exchange(v, axes):
    return lax.all_to_all(v, axes, 0, 0, tiled=True)


def swap(v):
    return lax.ppermute(v, "core", [(0, 1), (1, 0)])


def along_x(v, step):
    return lax.ppermute(v, "x", [(i, (i + step) % X) for i in range(X)])


def local(student_hidden, teacher_hidden, student_head, teacher_head):
    rows = student_head.shape[0]
    xi = lax.axis_index("x").reshape(1)
    s_heads = [student_head, swap(student_head)]
    t_heads = [teacher_head, swap(teacher_head)]

    message = call(
        message_kernel,
        array((Z * Y, PAD + HALF, FT), BF),
        student_hidden,
        teacher_hidden,
        anywhere=2,
        mib=60,
        scratch=[
            pltpu.VMEM((TOK, FS), BF),
            pltpu.VMEM((TOK, FT), BF),
            pltpu.VMEM((PAD, FS), F32),
            pltpu.VMEM((PAD, FT), F32),
            pltpu.SemaphoreType.DMA((2,)),
        ],
    )
    near = exchange(message, ("z", "yq", "yp")).reshape(Z, Y, PAD + HALF, FT)
    part = array((PART, ALL), BF)
    own = call(block_kernel, (part, part), near)
    before = [along_x(v, 1) for v in own]
    after = [along_x(v, -1) for v in own]
    far = [along_x(before[0], 1), along_x(after[1], -1)]

    logit = array((2, rows, ALL), F32)
    far_cols = array((2, rows, Y * FT), BF)
    ls, lt, far_s, far_t = call(
        early_kernel,
        (logit, logit, far_cols, far_cols),
        xi,
        *s_heads,
        *t_heads,
        *own,
        *after,
        *before,
        scalars=1,
        anywhere=6,
        mib=16,
        cheap=True,
        scratch=[
            pltpu.VMEM((D_T, ALL), BF),
            pltpu.VMEM((D_S, ALL), BF),
            pltpu.SemaphoreType.DMA((2 + 4 * Y,)),
        ],
    )
    ls, lt, stat = call(
        late_kernel,
        (logit, logit, array((Y * X, 8, SIDE), F32)),
        xi,
        *far,
        far_s,
        far_t,
        ls,
        lt,
        scalars=1,
        scratch=[pltpu.VMEM((Y * FT, ALL), BF), pltpu.VMEM((Y * FT, ALL), BF)],
        flops=8 * rows * ALL * Y * FT,
    )
    stat = exchange(stat, ("yq", "yp", "x"))
    stat = call(merge_kernel, array((Z, 8, SIDE), F32), stat)
    stat = exchange(stat, "z")
    grads, by_ypx, kl = call(
        grads_kernel,
        (array((2, rows, ALL), BF), array((YP * X, ALL, YQ * FS), BF), array((8, 128), F32)),
        stat,
        ls,
        lt,
        *s_heads,
        scratch=[pltpu.VMEM((ALL, D_S), F32)],
        flops=4 * rows * ALL * D_S,
    )
    full_s = call(
        fill_kernel,
        array((D_S, ALL), BF),
        xi,
        *own,
        *after,
        *far,
        *before,
        kl,
        scalars=1,
        anywhere=9,
        scratch=[pltpu.SemaphoreType.DMA],
    )
    sent = call(sent_kernel, array((rows, D_S + 128), BF), grads, full_s, kl, flops=2 * rows * ALL * D_S)
    packed = call(
        pack_kernel, array((Z * YQ, HALF, 2 * FS), BF), exchange(by_ypx, ("yp", "x")), sent, anywhere=1
    )
    hidden_grad = call(last_kernel, array((TOK, FS), F32), exchange(packed, ("z", "yq")))
    head_grad, loss = call(
        kept_kernel,
        (array((rows, D_S), BF), array((1, 1), F32)),
        grads,
        full_s,
        kl,
        swap(sent),
        flops=2 * rows * ALL * D_S,
    )
    return (loss.reshape(()), hidden_grad, head_grad)


def solution(mesh):
    fine = Mesh(mesh.devices.reshape(Z, 2, YQ, YP, X), ("z", "core", "yq", "yp", "x"))
    rows, cols = ("z", "core"), ("yq", "yp", "x")
    return jax.shard_map(
        local,
        mesh=fine,
        in_specs=(P(rows, cols), P(rows, cols), P(rows + cols, None), P(rows + cols, None)),
        out_specs=(P(), P(rows, cols), P(rows + cols, None)),
        check_vma=False,
    )
```

```python
import functools

import jax
import jax.numpy as jnp
from jax import lax
from jax.experimental import pallas as pl
from jax.experimental.pallas import tpu as pltpu
from jax.sharding import Mesh, PartitionSpec as P

BF = jnp.bfloat16
F32 = jnp.float32
Z, Y, X = 8, 8, 4
YP = 2
YQ = Y // YP
TOK, PAD = 30, 32
HALF = PAD // 2
SIDE = Z * HALF
ALL = 2 * SIDE
FS, FT = 64, 128
HY = Y // 2
PART = HY * (FT + FS)
D_S, D_T = X * Y * FS, X * Y * FT
NT = (((1,), (1,)), ((), ()))


def call(kernel, out, *args, scratch=(), mib=24, flops=0, scalars=0, anywhere=0, cheap=False):
    specs = [pl.BlockSpec(memory_space=pltpu.SMEM)] * scalars
    specs += [pl.BlockSpec(memory_space=pltpu.VMEM)] * (len(args) - scalars - anywhere)
    specs += [pl.BlockSpec(memory_space=pl.ANY)] * anywhere
    outs = jax.tree.map(lambda o: pl.BlockSpec(memory_space=pltpu.VMEM), out)
    size = sum(a.size * a.dtype.itemsize for a in args) + sum(
        o.size * o.dtype.itemsize for o in jax.tree.leaves(out)
    )
    return pl.pallas_call(
        kernel,
        out_shape=out,
        in_specs=specs,
        out_specs=outs,
        scratch_shapes=scratch,
        compiler_params=pltpu.CompilerParams(vmem_limit_bytes=mib << 20),
        cost_estimate=pl.CostEstimate(flops=flops, bytes_accessed=0 if cheap else size, transcendentals=0),
    )(*args)


def array(shape, dtype):
    return jax.ShapeDtypeStruct(shape, dtype)


def message_kernel(s_any, t_any, o_ref, s_in, t_in, s_pad, t_pad, sems):
    copies = [
        pltpu.make_async_copy(s_any, s_in, sems.at[0]),
        pltpu.make_async_copy(t_any, t_in, sems.at[1]),
    ]
    for c in copies:
        c.start()
    s_pad[...] = jnp.zeros_like(s_pad)
    t_pad[...] = jnp.zeros_like(t_pad)
    for c in copies:
        c.wait()
    s_pad[0:TOK, :] = s_in[...].astype(F32)
    t_pad[0:TOK, :] = t_in[...].astype(F32)
    s = jnp.concatenate([s_pad[0:HALF, :], s_pad[HALF:PAD, :]], axis=1).astype(BF)
    both = jnp.concatenate([t_pad[...].astype(BF), s], axis=0)
    for i in range(Z * Y):
        o_ref[i] = both


def block_kernel(g_ref, lo_ref, hi_ref):
    for y in range(Y):
        o_ref = lo_ref if y < HY else hi_ref
        row = (y % HY) * FT
        for h in range(2):
            t = g_ref[:, y, h * HALF : (h + 1) * HALF, :].reshape(SIDE, FT)
            o_ref[row : row + FT, h * SIDE : (h + 1) * SIDE] = t.T
        s = g_ref[:, y, PAD : PAD + HALF, :].reshape(SIDE, 2 * FS).T
        row = HY * FT + (y % HY) * FS
        for h in range(2):
            o_ref[row : row + FS, h * SIDE : (h + 1) * SIDE] = s[h * FS : (h + 1) * FS]


def merged(parts):
    n = parts.shape[0]
    m = parts[0, 0:4]
    for i in range(1, n):
        m = jnp.maximum(m, parts[i, 0:4])
    total = jnp.zeros_like(m)
    cross = jnp.zeros((2, m.shape[1]), F32)
    for i in range(n):
        w = jnp.exp(parts[i, 0:4] - m)
        total = total + w
        cross = cross + w[0:2] * parts[i, 4:6]
    return m + jnp.log(total), cross / total[0:2]


def rows_of(lse, cross):
    return jnp.concatenate([lse, cross, jnp.zeros((2, lse.shape[1]), F32)], axis=0)


def halves(v):
    return [v[:, 0:SIDE], v[:, SIDE:ALL]]


def early_kernel(x_ref, *refs):
    s_heads, t_heads, blocks = refs[0:2], refs[2:4], refs[4:10]
    ls_ref, lt_ref, far_s, far_t, full_t, full_s, sems = refs[10:]
    xi = x_ref[0]
    far = lax.rem(xi + 2, X)
    for i, step in enumerate((0, 1, 3)):
        x = lax.rem(xi + step, X)
        for y in range(Y):
            ref = blocks[2 * i + y // HY]
            row = HY * FT + (y % HY) * FS
            at = pl.multiple_of((y * X + x) * FS, FS)
            pltpu.make_async_copy(ref.at[row : row + FS, :], full_s.at[pl.ds(at, FS), :], sems.at[0]).start()
            row = (y % HY) * FT
            at = pl.multiple_of((y * X + x) * FT, FT)
            pltpu.make_async_copy(ref.at[row : row + FT, :], full_t.at[pl.ds(at, FT), :], sems.at[1]).start()
    parts = []
    for b in range(2):
        for y in range(Y):
            cols = slice(y * FT, (y + 1) * FT)
            at = pl.multiple_of((y * X + far) * FT, FT)
            parts.append((t_heads[b].at[:, pl.ds(at, FT)], far_t.at[b, :, cols]))
            at = pl.multiple_of((y * X + far // 2 * 2) * FS, FT)
            parts.append((s_heads[b].at[:, pl.ds(at, FT)], far_s.at[b, :, cols]))
    later = [pltpu.make_async_copy(src, dst, sems.at[2 + i]) for i, (src, dst) in enumerate(parts)]
    for c in later:
        c.start()
    for y in range(Y):
        at = pl.multiple_of((y * X + far) * FT, FT)
        full_t[pl.ds(at, FT), :] = jnp.zeros((FT, ALL), BF)
        at = pl.multiple_of((y * X + far) * FS, FS)
        full_s[pl.ds(at, FS), :] = jnp.zeros((FS, ALL), BF)
    arrived = full_s.at[0 : D_S // X * 3, :]
    pltpu.make_async_copy(arrived, arrived, sems.at[0]).wait()
    for b in range(2):
        ls_ref[b] = jnp.dot(s_heads[b][...], full_s[...], preferred_element_type=F32)
    arrived = full_t.at[0 : D_T // X * 3, :]
    pltpu.make_async_copy(arrived, arrived, sems.at[1]).wait()
    for b in range(2):
        lt_ref[b] = jnp.dot(t_heads[b][...], full_t[...], preferred_element_type=F32)
    for c in later:
        c.wait()


def late_kernel(x_ref, lo_ref, hi_ref, far_s, far_t, ls_in, lt_in, ls_ref, lt_ref, stat_ref, rows_s, rows_t):
    odd = lax.rem(x_ref[0], 2)
    rows_s[...] = jnp.zeros_like(rows_s)
    for y in range(Y):
        ref = (lo_ref, hi_ref)[y // HY]
        rows_t[y * FT : (y + 1) * FT, :] = ref[(y % HY) * FT : (y % HY + 1) * FT, :]
        row = HY * FT + (y % HY) * FS
        at = pl.multiple_of(y * FT + odd * FS, FS)
        rows_s[pl.ds(at, FS), :] = ref[row : row + FS, :]
    for b in range(2):
        lt_ref[b] = lt_in[b] + jnp.dot(far_t[b], rows_t[...], preferred_element_type=F32)
        ls_ref[b] = ls_in[b] + jnp.dot(far_s[b], rows_s[...], preferred_element_type=F32)
    mt = jnp.maximum(jnp.max(lt_ref[0], axis=0, keepdims=True), jnp.max(lt_ref[1], axis=0, keepdims=True))
    ms = jnp.maximum(jnp.max(ls_ref[0], axis=0, keepdims=True), jnp.max(ls_ref[1], axis=0, keepdims=True))
    sums = [0.0, 0.0, 0.0]
    for b in range(2):
        lt, ls = lt_ref[b], ls_ref[b]
        et = jnp.exp(lt - mt)
        new = (et, jnp.exp(ls - ms), et * (lt - ls))
        sums = [a + jnp.sum(v, axis=0, keepdims=True) for a, v in zip(sums, new)]
    lse = halves(mt + jnp.log(sums[0])) + halves(ms + jnp.log(sums[1]))
    stat = rows_of(jnp.concatenate(lse, axis=0), jnp.concatenate(halves(sums[2] / sums[0]), axis=0))
    for i in range(Y * X):
        stat_ref[i] = stat


def fill_kernel(x_ref, *refs):
    blocks, o_ref, sem = refs[0:8], refs[9], refs[10]
    for step in range(X):
        x = lax.rem(x_ref[0] + step, X)
        for y in range(Y):
            ref = blocks[2 * step + y // HY]
            row = HY * FT + (y % HY) * FS
            at = pl.multiple_of((y * X + x) * FS, FS)
            pltpu.make_async_copy(ref.at[row : row + FS, :], o_ref.at[pl.ds(at, FS), :], sem).start()
    pltpu.make_async_copy(o_ref, o_ref, sem).wait()


def merge_kernel(p_ref, o_ref):
    stat = rows_of(*merged(p_ref))
    for i in range(Z):
        o_ref[i] = stat


def grads_kernel(p_ref, ls_ref, lt_ref, s0_ref, s1_ref, g_ref, by_ypx_ref, kl_ref, terms):
    lse, cross = merged(p_ref)
    lse_t = jnp.concatenate([lse[0:1], lse[1:2]], axis=1)
    lse_s = jnp.concatenate([lse[2:3], lse[3:4]], axis=1)
    kl = jnp.concatenate([cross[0:1], cross[1:2]], axis=1) - lse_t + lse_s
    lane = lax.broadcasted_iota(jnp.int32, (1, ALL), 1)
    padding = (lane >= SIDE) & ((lane & (HALF - 1)) >= TOK - HALF)
    kl_ref[...] = jnp.broadcast_to(jnp.sum(jnp.where(padding, 0.0, kl), axis=1, keepdims=True), kl_ref.shape)
    for b, head in enumerate((s0_ref, s1_ref)):
        g = (jnp.exp(ls_ref[b] - lse_s) - jnp.exp(lt_ref[b] - lse_t)).astype(BF)
        g_ref[b] = g
        part = lax.dot_general(g, head[...], (((0,), (0,)), ((), ())), preferred_element_type=F32)
        terms[...] = part if b == 0 else terms[...] + part
    for yp in range(YP):
        for x in range(X):
            for q in range(YQ // 2):
                ys = [(2 * q + i) * YP + yp for i in range(2)]
                pair = [terms[:, (y * X + x) * FS : (y * X + x + 1) * FS] for y in ys]
                by_ypx_ref[yp * X + x, :, q * 2 * FS : (q + 1) * 2 * FS] = jnp.concatenate(pair, axis=1).astype(BF)


def thirds(v):
    hi = v.astype(BF)
    mid = (v - hi.astype(F32)).astype(BF)
    return hi, mid, (v - hi.astype(F32) - mid.astype(F32)).astype(BF)


def sent_kernel(g_ref, full_s, kl_ref, o_ref):
    o_ref[:, 0:D_S] = lax.dot_general(g_ref[1], full_s[...], NT, preferred_element_type=F32).astype(BF)
    lane = lax.broadcasted_iota(jnp.int32, (1, 128), 1)
    row = jnp.zeros((1, 128), F32)
    for i, v in enumerate(thirds(kl_ref[0:1, :])):
        row = jnp.where(lane == i, v.astype(F32), row)
    o_ref[:, D_S : D_S + 128] = jnp.broadcast_to(row, (o_ref.shape[0], 128)).astype(BF)


def kept_kernel(g_ref, full_s, kl_ref, arrived, o_ref, loss_ref):
    kept = lax.dot_general(g_ref[0], full_s[...], NT, preferred_element_type=F32)
    o_ref[...] = (kept + arrived[:, 0:D_S].astype(F32)).astype(BF)
    hi, mid, lo = [v.astype(F32) for v in thirds(kl_ref[0:1, 0:1])]
    other = arrived[0:16, D_S : D_S + 128].astype(F32)[0:1]
    there = other[:, 0:1] + other[:, 1:2] + other[:, 2:3]
    loss_ref[...] = (hi + mid + lo + there) / (2 * Z * TOK)


def pack_kernel(r_ref, _, o_ref):
    row = r_ref[0].astype(F32)
    for i in range(1, YP * X):
        row = row + r_ref[i].astype(F32)
    for z in range(Z):
        sides = [row[h * SIDE + z * HALF : h * SIDE + (z + 1) * HALF] for h in range(2)]
        for yq in range(YQ):
            pair = [v[:, yq * FS : (yq + 1) * FS] for v in sides]
            o_ref[z * YQ + yq] = jnp.concatenate(pair, axis=1).astype(BF)


def last_kernel(r_ref, o_ref):
    total = jnp.sum(r_ref[...].astype(F32), axis=0)
    o_ref[0:HALF, :] = total[:, 0:FS]
    o_ref[HALF:TOK, :] = total[0 : TOK - HALF, FS : 2 * FS]


def exchange(v, axes):
    return lax.all_to_all(v, axes, 0, 0, tiled=True)


def swap(v):
    return lax.ppermute(v, "core", [(0, 1), (1, 0)])


def along_x(v, step):
    return lax.ppermute(v, "x", [(i, (i + step) % X) for i in range(X)])


def local(student_hidden, teacher_hidden, student_head, teacher_head):
    rows = student_head.shape[0]
    xi = lax.axis_index("x").reshape(1)
    s_heads = [student_head, swap(student_head)]
    t_heads = [teacher_head, swap(teacher_head)]

    message = call(
        message_kernel,
        array((Z * Y, PAD + HALF, FT), BF),
        student_hidden,
        teacher_hidden,
        anywhere=2,
        mib=60,
        scratch=[
            pltpu.VMEM((TOK, FS), BF),
            pltpu.VMEM((TOK, FT), BF),
            pltpu.VMEM((PAD, FS), F32),
            pltpu.VMEM((PAD, FT), F32),
            pltpu.SemaphoreType.DMA((2,)),
        ],
    )
    near = exchange(message, ("z", "yq", "yp")).reshape(Z, Y, PAD + HALF, FT)
    part = array((PART, ALL), BF)
    own = call(block_kernel, (part, part), near)
    before = [along_x(v, 1) for v in own]
    after = [along_x(v, -1) for v in own]
    far = [along_x(before[0], 1), along_x(after[1], -1)]

    logit = array((2, rows, ALL), F32)
    far_cols = array((2, rows, Y * FT), BF)
    ls, lt, far_s, far_t = call(
        early_kernel,
        (logit, logit, far_cols, far_cols),
        xi,
        *s_heads,
        *t_heads,
        *own,
        *after,
        *before,
        scalars=1,
        anywhere=6,
        mib=16,
        cheap=True,
        scratch=[
            pltpu.VMEM((D_T, ALL), BF),
            pltpu.VMEM((D_S, ALL), BF),
            pltpu.SemaphoreType.DMA((2 + 4 * Y,)),
        ],
    )
    ls, lt, stat = call(
        late_kernel,
        (logit, logit, array((Y * X, 8, SIDE), F32)),
        xi,
        *far,
        far_s,
        far_t,
        ls,
        lt,
        scalars=1,
        scratch=[pltpu.VMEM((Y * FT, ALL), BF), pltpu.VMEM((Y * FT, ALL), BF)],
        flops=8 * rows * ALL * Y * FT,
    )
    stat = exchange(stat, ("yq", "yp", "x"))
    stat = call(merge_kernel, array((Z, 8, SIDE), F32), stat)
    stat = exchange(stat, "z")
    grads, by_ypx, kl = call(
        grads_kernel,
        (array((2, rows, ALL), BF), array((YP * X, ALL, YQ * FS), BF), array((8, 128), F32)),
        stat,
        ls,
        lt,
        *s_heads,
        scratch=[pltpu.VMEM((ALL, D_S), F32)],
        flops=4 * rows * ALL * D_S,
    )
    full_s = call(
        fill_kernel,
        array((D_S, ALL), BF),
        xi,
        *own,
        *after,
        *far,
        *before,
        kl,
        scalars=1,
        anywhere=9,
        scratch=[pltpu.SemaphoreType.DMA],
    )
    sent = call(sent_kernel, array((rows, D_S + 128), BF), grads, full_s, kl, flops=2 * rows * ALL * D_S)
    packed = call(
        pack_kernel, array((Z * YQ, HALF, 2 * FS), BF), exchange(by_ypx, ("yp", "x")), sent, anywhere=1, mib=60
    )
    hidden_grad = call(last_kernel, array((TOK, FS), F32), exchange(packed, ("z", "yq")))
    head_grad, loss = call(
        kept_kernel,
        (array((rows, D_S), BF), array((1, 1), F32)),
        grads,
        full_s,
        kl,
        swap(sent),
        flops=2 * rows * ALL * D_S,
    )
    return (loss.reshape(()), hidden_grad, head_grad)


def solution(mesh):
    fine = Mesh(mesh.devices.reshape(Z, 2, YQ, YP, X), ("z", "core", "yq", "yp", "x"))
    rows, cols = ("z", "core"), ("yq", "yp", "x")
    return jax.shard_map(
        local,
        mesh=fine,
        in_specs=(P(rows, cols), P(rows, cols), P(rows + cols, None), P(rows + cols, None)),
        out_specs=(P(), P(rows, cols), P(rows + cols, None)),
        check_vma=False,
    )
```
